512 devices in a mesh: row: 32 (over y_hi, z, core), col: 4 (over y_lo), dp: 4 (over x).
Axes of the slice: x: 4, y: 8 (y_hi: 2, y_lo: 4; y = y_hi * 4 + y_lo), z: 8, core: 2. Of those that a mesh axis runs over, the one named last changes fastest.
Arguments:
- activations: bfloat16 [2048, 8192], P('dp', 'row'), may hold values from -6 to 6
- out_grads: bfloat16 [2048, 14336], P('dp', 'col'), may hold values from -0.5390625 to 0.5390625
- projector: bfloat16 [8192, 256], P('row'), may hold values from -0.125 to 0.125
- weight: bfloat16 [8192, 14336], P('row', ('col', 'dp')), may hold values from -6 to 6
- moment: float32 [256, 14336], P('row', ('col', 'dp')), may hold values from -1.8 to 1.8
- second: float32 [256, 14336], P('row', ('col', 'dp')), may hold values from 0.0001 to 0.01
Outputs:
- new_weight: bfloat16 [8192, 14336], P('row', ('col', 'dp'))
- new_moment: float32 [256, 14336], P('row', ('col', 'dp'))
- new_second: float32 [256, 14336], P('row', ('col', 'dp'))
The draws below stay inside these ranges and needn't reach their ends.
All inputs are finite; a program needn't handle non-finite values.
Results may differ from the reference program's by a relative error of at most 0.0034.
Values may be sent and summed in bfloat16 or wider, within the bound.
A program may use at most 64 MiB of HBM per device.

```python
import math
import jax
import jax.numpy as jnp
from jax import lax

H = 8192
F = 14336
R = 256
TOKENS = 2048
N_DP = 4


def with_spikes(entries, stream_key, source, target, blocks, factor):
    def block_of(position):
        return (jnp.arange(entries.shape[position]) // (entries.shape[position] // blocks)).reshape((-1,) + (1,) * (entries.ndim - 1 - position))

    near = jax.random.permutation(stream_key, blocks)[block_of(target)]
    far = (block_of(target) + blocks // 2) % blocks
    return jnp.where((block_of(source) == near) | (block_of(source) == far), factor * entries, entries)


def level_of(key, shape, pieces, smallest, top_value):
    level, own = 1.0, jax.random.fold_in(key, 6)
    for axis_at, shards_of in pieces:
        heights = jnp.exp(jax.random.uniform(jax.random.fold_in(own, axis_at), (shards_of,), jnp.float32, smallest / len(pieces), top_value / len(pieces)))
        level = level * jnp.repeat(heights, shape[axis_at] // shards_of).reshape([-1 if axis == axis_at else 1 for axis in range(len(shape))])
    return level


def noise(stream_key, shape, width, reach, cuts=(), dtype=jnp.bfloat16):
    level = level_of(stream_key, shape, cuts, -0.22, 0.18) if cuts else 1.0
    array = jax.random.normal(stream_key, shape, jnp.float32) * width * level
    return jnp.minimum(jnp.maximum(array, -reach), reach).astype(dtype)


def bell_draw_with(own_key, shape, scale, reach, pieces, heavy, held_as=jnp.bfloat16):
    drawn = scale * jax.random.normal(own_key, shape, jnp.float32)
    if pieces:
        drawn = drawn * level_of(own_key, shape, pieces, -0.22, 0.18)
    return jnp.clip(with_spikes(drawn, jax.random.fold_in(own_key, 3), *heavy), -reach, reach).astype(held_as)


def setup_inputs(seed: int = 0) -> dict:
    streams_of = jax.random.split(jax.random.key(seed), 7)
    activations = noise(streams_of[0], (TOKENS, H), 1.0, 6.0, ((0, 4), (1, 32)))
    out_grads = noise(streams_of[1], (TOKENS, F), 0.09, 0.5390625, ((0, 4), (1, 4)))
    projector = bell_draw_with(streams_of[2], (H, R), H ** -0.5, 0.125, ((0, 32),), (0, 1, 32, 2.75))
    weight = noise(streams_of[3], (H, F), 1.0, 6.0, ((0, 32), (1, 16)))
    moment = noise(streams_of[4], (R, F), 0.3, 1.8, ((0, 32), (1, 16)), jnp.float32)
    second = jnp.clip(jnp.exp(math.log(0.01) - 4.6051702 * jax.random.uniform(streams_of[5], (R, F), jnp.float32) ** level_of(streams_of[5], (R, F), ((0, 32), (1, 16)), -0.2, 0.2)), 0.0001, 0.01)
    return {"activations": activations, "out_grads": out_grads, "projector": projector, "weight": weight, "moment": moment, "second": second}


def reference(activations, out_grads, projector, weight, moment, second):
    coords = jnp.dot(activations.astype(jnp.float32), projector.astype(jnp.float32), precision=lax.Precision.HIGHEST)
    low = jnp.dot(coords.T, out_grads.astype(jnp.float32), precision=lax.Precision.HIGHEST) * (1.0 / N_DP)
    new_moment = 0.9 * moment + 0.1 * low
    new_second = 0.999 * second + 0.001 * low * low
    first_fix = 1.0 / (1.0 - 0.9 ** 10)
    second_fix = 1.0 / (1.0 - 0.999 ** 10)
    direction = (new_moment * first_fix / (jnp.sqrt(new_second * second_fix) + 1e-08)).astype(jnp.bfloat16)
    update = jnp.dot(projector.astype(jnp.float32), direction.astype(jnp.float32), precision=lax.Precision.HIGHEST)
    new_weight = (weight.astype(jnp.float32) - 0.5 * update).astype(jnp.bfloat16)
    return (new_weight, new_moment, new_second)
```

```python
import jax
import jax.numpy as jnp
from jax import lax
from jax.experimental import pallas as pl
from jax.experimental.pallas import tpu as pltpu
from jax.sharding import PartitionSpec as P

MESH = pl.DeviceIdType.MESH
A_TYPE = jnp.float32
D_TYPE = jnp.float32

NZ, NK, NYH, NYL, NX = 8, 2, 2, 4, 4
NQ, NY = NZ * NK, NYH * NYL
OWN = 8
TOK = 128
R = 256
COLS = 896
FAR_FIRST = (4, 3, 5, 2, 6, 1, 7)
NEAR_FIRST = (1, 7, 2, 6, 3, 5, 4)
FIRST_FIX = 1.0 / (1.0 - 0.9**10)
SECOND_FIX = 1.0 / (1.0 - 0.999**10)


def kernel(
    act, grads, proj, weight, moment, second,
    new_weight, new_moment, new_second,
    act_v, proj_v, perm_v, grads_v, weight_v, mv, state_v, out_v,
    send_a, recv_a, recv_b, send_d, recv_d, dirs, low_v,
    in_sem, out_sem, mv_sem, a_sem, b_sem, d_sem, f_sem, c_sem,
):
    row, col, dp = lax.axis_index("row"), lax.axis_index("col"), lax.axis_index("dp")
    yh, z, k = row // NQ, (row // NK) % NZ, row % NK
    y, q = yh * NYL + col, row % NQ

    def at_zk(dz, dk):
        return (yh * NQ + ((z + dz) % NZ) * NK + (k + dk) % NK, col, dp)

    def at_y(dy):
        to = (y + dy) % NY
        return ((to // NYL) * NQ + q, to % NYL, dp)

    def at_x(dx):
        return (row, col, (dp + dx) % NX)

    zk = [(dz, dk) for dz in FAR_FIRST for dk in range(NK)] + [(0, 1)]

    loads = [
        pltpu.make_async_copy(act.at[pl.ds(pl.multiple_of(col * TOK, TOK), TOK), :], act_v, in_sem.at[0]),
        pltpu.make_async_copy(proj, proj_v, in_sem.at[1]),
        pltpu.make_async_copy(moment, mv.at[yh, 0], in_sem.at[2]),
        pltpu.make_async_copy(second, mv.at[yh, 1], in_sem.at[3]),
    ]
    for x in range(NX):
        loads.append(pltpu.make_async_copy(grads.at[:, pl.ds(x * COLS, COLS)], grads_v.at[x], in_sem.at[4 + x]))
    loads.append(pltpu.make_async_copy(weight, weight_v, in_sem.at[8]))
    for load in loads[:2]:
        load.start()

    barrier = pltpu.get_barrier_semaphore()
    peers = [at_zk(dz, dk) for dz, dk in zk] + [at_y(dy) for dy in FAR_FIRST] + [at_x(dx) for dx in (2, 1, 3)]
    for peer in peers:
        pl.semaphore_signal(barrier, inc=1, device_id=peer, device_id_type=MESH)
    for load in loads[2:]:
        load.start()

    loads[0].wait()
    loads[1].wait()
    part = lax.dot_general(proj_v[...], act_v[...], (((0,), (1,)), ((), ())), preferred_element_type=jnp.float32)
    part = part.reshape(NYH, NQ, OWN, TOK)
    send_a[...] = jnp.concatenate([part[0], part[1]], axis=1).astype(A_TYPE)

    pl.semaphore_wait(barrier, len(peers))
    copies = []

    sends_a = []
    for j, (dz, dk) in enumerate(zk):
        to = ((z + dz) % NZ) * NK + (k + dk) % NK
        copy = pltpu.make_async_remote_copy(
            src_ref=send_a.at[to], dst_ref=recv_a.at[j], send_sem=a_sem.at[0, j], recv_sem=a_sem.at[1, j],
            device_id=at_zk(dz, dk), device_id_type=MESH,
        )
        copy.start()
        sends_a.append(copy)

    loads[2].wait()
    loads[3].wait()
    send_mv = pltpu.make_async_remote_copy(
        src_ref=mv.at[yh], dst_ref=mv.at[yh], send_sem=mv_sem.at[0], recv_sem=mv_sem.at[1],
        device_id=at_y(NYL), device_id_type=MESH,
    )
    send_mv.start()

    source = lax.broadcasted_iota(jnp.int32, (R, R), 0)
    place = lax.broadcasted_iota(jnp.int32, (R, R), 1)
    wanted = (place % (NYH * OWN)) // OWN * (NQ * OWN) + place // (NYH * OWN) * OWN + place % OWN
    shuffle = jnp.where(source == wanted, 1.0, 0.0).astype(jnp.bfloat16)
    perm_v[...] = jnp.dot(proj_v[...], shuffle, preferred_element_type=jnp.float32).astype(jnp.bfloat16)

    total = send_a[q].astype(jnp.float32)
    for j in reversed(range(len(zk))):
        sends_a[j].wait_recv()
        total += recv_a[j].astype(jnp.float32)

    recv_b[y] = total
    sends_b = []
    for j, dy in enumerate(FAR_FIRST):
        copy = pltpu.make_async_remote_copy(
            src_ref=recv_b.at[y], dst_ref=recv_b.at[y], send_sem=b_sem.at[0, j], recv_sem=b_sem.at[1, j],
            device_id=at_y(dy), device_id_type=MESH,
        )
        copy.start()
        sends_b.append(copy)
    for load in loads[4:8]:
        load.wait()
    for copy in sends_b:
        copy.wait_recv()
    coords = jnp.concatenate([recv_b[c] + recv_b[NYL + c] for c in range(NYL)], axis=1)
    high = coords.astype(jnp.bfloat16)
    rest = (coords - high.astype(jnp.float32)).astype(jnp.bfloat16)
    both = jnp.concatenate([high, rest], axis=0)

    def low_of(to):
        product = jnp.dot(both, grads_v[to], preferred_element_type=jnp.float32)
        return product[: NYH * OWN] + product[NYH * OWN :]

    sends_d = []
    for j, dx in enumerate((2, 1, 3)):
        send_d[j] = low_of((dp + dx) % NX).astype(D_TYPE)
        copy = pltpu.make_async_remote_copy(
            src_ref=send_d.at[j], dst_ref=recv_d.at[j], send_sem=d_sem.at[0, j], recv_sem=d_sem.at[1, j],
            device_id=at_x(dx), device_id_type=MESH,
        )
        copy.start()
        sends_d.append(copy)
    low_v[...] = low_of(dp)
    send_mv.wait_recv()
    for copy in sends_d:
        copy.wait_recv()
    low = low_v[...] + recv_d[1].astype(jnp.float32) + recv_d[2].astype(jnp.float32) + recv_d[0].astype(jnp.float32)
    low = (low * (1.0 / NX)).reshape(NYH, OWN, COLS)
    state_m = 0.9 * mv[:, 0] + 0.1 * low
    state_s = 0.999 * mv[:, 1] + 0.001 * low * low
    direction = state_m * FIRST_FIX / (jnp.sqrt(state_s * SECOND_FIX) + 1e-08)
    dirs[q] = direction.reshape(NYH * OWN, COLS).astype(jnp.bfloat16)

    sends_f = []
    for j, dz in enumerate(FAR_FIRST):
        copy = pltpu.make_async_remote_copy(
            src_ref=dirs.at[q], dst_ref=dirs.at[q], send_sem=f_sem.at[0, j], recv_sem=f_sem.at[1, j],
            device_id=at_zk(dz, 0), device_id_type=MESH,
        )
        copy.start()
        sends_f.append(copy)

    def to_other_core(block, j):
        copy = pltpu.make_async_remote_copy(
            src_ref=dirs.at[block], dst_ref=dirs.at[block], send_sem=c_sem.at[0, j], recv_sem=c_sem.at[1, j],
            device_id=at_zk(0, 1), device_id_type=MESH,
        )
        copy.start()
        return copy

    sends_c = [to_other_core(q, 0)]
    state_v[0] = state_m
    state_v[1] = state_s
    stores = [
        pltpu.make_async_copy(state_v.at[0, yh], new_moment, out_sem.at[0]),
        pltpu.make_async_copy(state_v.at[1, yh], new_second, out_sem.at[1]),
    ]
    for store in stores:
        store.start()
    loads[8].wait()
    for j, dz in enumerate(NEAR_FIRST):
        sends_f[FAR_FIRST.index(dz)].wait_recv()
        sends_c.append(to_other_core(((z - dz + NZ) % NZ) * NK + k, 1 + j))
    for copy in sends_c:
        copy.wait_recv()

    update = jnp.dot(perm_v[...], dirs[...].reshape(R, COLS), preferred_element_type=jnp.float32)
    out_v[...] = (weight_v[...].astype(jnp.float32) - 0.5 * update).astype(jnp.bfloat16)
    store = pltpu.make_async_copy(out_v, new_weight, out_sem.at[2])
    store.start()
    for copy in sends_a + [send_mv] + sends_b + sends_d + sends_f + sends_c:
        copy.wait_send()
    for copy in stores + [store]:
        copy.wait()


def per_device(activations, out_grads, projector, weight, moment, second):
    any_space = pl.BlockSpec(memory_space=pl.ANY)
    return pl.pallas_call(
        kernel,
        out_shape=(
            jax.ShapeDtypeStruct(weight.shape, jnp.bfloat16),
            jax.ShapeDtypeStruct(moment.shape, jnp.float32),
            jax.ShapeDtypeStruct(second.shape, jnp.float32),
        ),
        in_specs=[any_space] * 6,
        out_specs=[any_space] * 3,
        scratch_shapes=[
            pltpu.VMEM((TOK, 256), jnp.bfloat16),
            pltpu.VMEM((256, R), jnp.bfloat16),
            pltpu.VMEM((256, R), jnp.bfloat16),
            pltpu.VMEM((NX, 512, COLS), jnp.bfloat16),
            pltpu.VMEM((256, COLS), jnp.bfloat16),
            pltpu.VMEM((NYH, 2, OWN, COLS), jnp.float32),
            pltpu.VMEM((2, NYH, OWN, COLS), jnp.float32),
            pltpu.VMEM((256, COLS), jnp.bfloat16),
            pltpu.VMEM((NQ, NYH * OWN, TOK), A_TYPE),
            pltpu.VMEM((NQ, NYH * OWN, TOK), A_TYPE),
            pltpu.VMEM((NY, NYH * OWN, TOK), jnp.float32),
            pltpu.VMEM((NX - 1, NYH * OWN, COLS), D_TYPE),
            pltpu.VMEM((NX - 1, NYH * OWN, COLS), D_TYPE),
            pltpu.VMEM((NQ, NYH * OWN, COLS), jnp.bfloat16),
            pltpu.VMEM((NYH * OWN, COLS), jnp.float32),
            pltpu.SemaphoreType.DMA((9,)),
            pltpu.SemaphoreType.DMA((3,)),
            pltpu.SemaphoreType.DMA((2,)),
            pltpu.SemaphoreType.DMA((2, NQ)),
            pltpu.SemaphoreType.DMA((2, NY)),
            pltpu.SemaphoreType.DMA((2, NX)),
            pltpu.SemaphoreType.DMA((2, NZ)),
            pltpu.SemaphoreType.DMA((2, NZ)),
        ],
        compiler_params=pltpu.CompilerParams(
            collective_id=0, has_side_effects=True, vmem_limit_bytes=60 * 1024 * 1024
        ),
        name="galore_step",
    )(activations, out_grads, projector, weight, moment, second)


def solution(mesh):
    in_specs = (
        P("dp", "row"),
        P("dp", "col"),
        P("row", None),
        P("row", ("col", "dp")),
        P("row", ("col", "dp")),
        P("row", ("col", "dp")),
    )
    out_specs = (P("row", ("col", "dp")), P("row", ("col", "dp")), P("row", ("col", "dp")))
    return jax.shard_map(
        per_device, mesh=mesh, in_specs=in_specs, out_specs=out_specs, check_vma=False
    )
```

```python
import jax
import jax.numpy as jnp
from jax import lax
from jax.experimental import pallas as pl
from jax.experimental.pallas import tpu as pltpu
from jax.sharding import PartitionSpec as P

MESH = pl.DeviceIdType.MESH
A_TYPE = jnp.float32
D_TYPE = jnp.float32

NZ, NK, NYH, NYL, NX = 8, 2, 2, 4, 4
NQ, NY = NZ * NK, NYH * NYL
OWN = 8
TOK = 128
R = 256
COLS = 896
FAR_FIRST = (4, 3, 5, 2, 6, 1, 7)
NEAR_FIRST = (1, 7, 2, 6, 3, 5, 4)
FIRST_FIX = 1.0 / (1.0 - 0.9**10)
SECOND_FIX = 1.0 / (1.0 - 0.999**10)


def kernel(
    act, grads, proj, weight, moment, second,
    dirs, perm_v, weight_v, state_v,
    act_v, proj_v, grads_v, mv, send_a, recv_a, recv_b, send_d, recv_d, low_v,
    in_sem, mv_sem, a_sem, b_sem, d_sem, f_sem, c_sem,
):
    row, col, dp = lax.axis_index("row"), lax.axis_index("col"), lax.axis_index("dp")
    yh, z, k = row // NQ, (row // NK) % NZ, row % NK
    y, q = yh * NYL + col, row % NQ

    def at_zk(dz, dk):
        return (yh * NQ + ((z + dz) % NZ) * NK + (k + dk) % NK, col, dp)

    def at_y(dy):
        to = (y + dy) % NY
        return ((to // NYL) * NQ + q, to % NYL, dp)

    def at_x(dx):
        return (row, col, (dp + dx) % NX)

    zk = [(dz, dk) for dz in FAR_FIRST for dk in range(NK)] + [(0, 1)]

    loads = [
        pltpu.make_async_copy(act.at[pl.ds(pl.multiple_of(col * TOK, TOK), TOK), :], act_v, in_sem.at[0]),
        pltpu.make_async_copy(proj, proj_v, in_sem.at[1]),
        pltpu.make_async_copy(moment, mv.at[yh, 0], in_sem.at[2]),
        pltpu.make_async_copy(second, mv.at[yh, 1], in_sem.at[3]),
    ]
    for x in range(NX):
        loads.append(pltpu.make_async_copy(grads.at[:, pl.ds(x * COLS, COLS)], grads_v.at[x], in_sem.at[4 + x]))
    loads.append(pltpu.make_async_copy(weight, weight_v, in_sem.at[8]))
    for load in loads[:2]:
        load.start()

    barrier = pltpu.get_barrier_semaphore()
    peers = [at_zk(dz, dk) for dz, dk in zk] + [at_y(dy) for dy in FAR_FIRST] + [at_x(dx) for dx in (2, 1, 3)]
    for peer in peers:
        pl.semaphore_signal(barrier, inc=1, device_id=peer, device_id_type=MESH)
    for load in loads[2:]:
        load.start()

    loads[0].wait()
    loads[1].wait()
    part = lax.dot_general(proj_v[...], act_v[...], (((0,), (1,)), ((), ())), preferred_element_type=jnp.float32)
    part = part.reshape(NYH, NQ, OWN, TOK)
    send_a[...] = jnp.concatenate([part[0], part[1]], axis=1).astype(A_TYPE)

    pl.semaphore_wait(barrier, len(peers))
    copies = []

    sends_a = []
    for j, (dz, dk) in enumerate(zk):
        to = ((z + dz) % NZ) * NK + (k + dk) % NK
        copy = pltpu.make_async_remote_copy(
            src_ref=send_a.at[to], dst_ref=recv_a.at[j], send_sem=a_sem.at[0, j], recv_sem=a_sem.at[1, j],
            device_id=at_zk(dz, dk), device_id_type=MESH,
        )
        copy.start()
        sends_a.append(copy)

    loads[2].wait()
    loads[3].wait()
    send_mv = pltpu.make_async_remote_copy(
        src_ref=mv.at[yh], dst_ref=mv.at[yh], send_sem=mv_sem.at[0], recv_sem=mv_sem.at[1],
        device_id=at_y(NYL), device_id_type=MESH,
    )
    send_mv.start()

    source = lax.broadcasted_iota(jnp.int32, (R, R), 0)
    place = lax.broadcasted_iota(jnp.int32, (R, R), 1)
    wanted = (place % (NYH * OWN)) // OWN * (NQ * OWN) + place // (NYH * OWN) * OWN + place % OWN
    shuffle = jnp.where(source == wanted, 1.0, 0.0).astype(jnp.bfloat16)
    perm_v[...] = jnp.dot(proj_v[...], shuffle, preferred_element_type=jnp.float32).astype(jnp.bfloat16)

    total = send_a[q].astype(jnp.float32)
    for j in reversed(range(len(zk))):
        sends_a[j].wait_recv()
        total += recv_a[j].astype(jnp.float32)

    recv_b[y] = total
    sends_b = []
    for j, dy in enumerate(FAR_FIRST):
        copy = pltpu.make_async_remote_copy(
            src_ref=recv_b.at[y], dst_ref=recv_b.at[y], send_sem=b_sem.at[0, j], recv_sem=b_sem.at[1, j],
            device_id=at_y(dy), device_id_type=MESH,
        )
        copy.start()
        sends_b.append(copy)
    for load in loads[4:8]:
        load.wait()
    for copy in sends_b:
        copy.wait_recv()
    coords = jnp.concatenate([recv_b[c] + recv_b[NYL + c] for c in range(NYL)], axis=1)
    high = coords.astype(jnp.bfloat16)
    rest = (coords - high.astype(jnp.float32)).astype(jnp.bfloat16)
    both = jnp.concatenate([high, rest], axis=0)

    def low_of(to):
        product = jnp.dot(both, grads_v[to], preferred_element_type=jnp.float32)
        return product[: NYH * OWN] + product[NYH * OWN :]

    sends_d = []
    for j, dx in enumerate((2, 1, 3)):
        send_d[j] = low_of((dp + dx) % NX).astype(D_TYPE)
        copy = pltpu.make_async_remote_copy(
            src_ref=send_d.at[j], dst_ref=recv_d.at[j], send_sem=d_sem.at[0, j], recv_sem=d_sem.at[1, j],
            device_id=at_x(dx), device_id_type=MESH,
        )
        copy.start()
        sends_d.append(copy)
    low_v[...] = low_of(dp)
    send_mv.wait_recv()
    for copy in sends_d:
        copy.wait_recv()
    low = low_v[...] + recv_d[1].astype(jnp.float32) + recv_d[2].astype(jnp.float32) + recv_d[0].astype(jnp.float32)
    low = (low * (1.0 / NX)).reshape(NYH, OWN, COLS)
    state_m = 0.9 * mv[:, 0] + 0.1 * low
    state_s = 0.999 * mv[:, 1] + 0.001 * low * low
    direction = state_m * FIRST_FIX / (jnp.sqrt(state_s * SECOND_FIX) + 1e-08)
    dirs[q] = direction.reshape(NYH * OWN, COLS).astype(jnp.bfloat16)

    sends_f = []
    for j, dz in enumerate(FAR_FIRST):
        copy = pltpu.make_async_remote_copy(
            src_ref=dirs.at[q], dst_ref=dirs.at[q], send_sem=f_sem.at[0, j], recv_sem=f_sem.at[1, j],
            device_id=at_zk(dz, 0), device_id_type=MESH,
        )
        copy.start()
        sends_f.append(copy)

    def to_other_core(block, j):
        copy = pltpu.make_async_remote_copy(
            src_ref=dirs.at[block], dst_ref=dirs.at[block], send_sem=c_sem.at[0, j], recv_sem=c_sem.at[1, j],
            device_id=at_zk(0, 1), device_id_type=MESH,
        )
        copy.start()
        return copy

    sends_c = [to_other_core(q, 0)]
    state_v[0] = jnp.where(yh == 0, state_m[0], state_m[1])
    state_v[1] = jnp.where(yh == 0, state_s[0], state_s[1])
    loads[8].wait()
    for j, dz in enumerate(NEAR_FIRST):
        sends_f[FAR_FIRST.index(dz)].wait_recv()
        sends_c.append(to_other_core(((z - dz + NZ) % NZ) * NK + k, 1 + j))
    for copy in sends_c:
        copy.wait_recv()

    for copy in sends_a + [send_mv] + sends_b + sends_d + sends_f + sends_c:
        copy.wait_send()


def finish(dirs, perm, weight, state, new_weight, new_moment, new_second, out_v, out_sem):
    stores = [
        pltpu.make_async_copy(state.at[0], new_moment, out_sem.at[0]),
        pltpu.make_async_copy(state.at[1], new_second, out_sem.at[1]),
    ]
    for store in stores:
        store.start()
    update = jnp.dot(perm[...], dirs[...].reshape(R, COLS), preferred_element_type=jnp.float32)
    out_v[...] = (weight[...].astype(jnp.float32) - 0.5 * update).astype(jnp.bfloat16)
    stores.append(pltpu.make_async_copy(out_v, new_weight, out_sem.at[2]))
    stores[2].start()
    for store in stores:
        store.wait()


def per_device(activations, out_grads, projector, weight, moment, second):
    any_space = pl.BlockSpec(memory_space=pl.ANY)
    vmem = pl.BlockSpec(memory_space=pltpu.VMEM)
    held = pl.pallas_call(
        kernel,
        out_shape=(
            pltpu.VMEM((NQ, NYH * OWN, COLS), jnp.bfloat16),
            pltpu.VMEM((256, R), jnp.bfloat16),
            pltpu.VMEM((256, COLS), jnp.bfloat16),
            pltpu.VMEM((2, OWN, COLS), jnp.float32),
        ),
        in_specs=[any_space] * 6,
        out_specs=[vmem] * 4,
        scratch_shapes=[
            pltpu.VMEM((TOK, 256), jnp.bfloat16),
            pltpu.VMEM((256, R), jnp.bfloat16),
            pltpu.VMEM((NX, 512, COLS), jnp.bfloat16),
            pltpu.VMEM((NYH, 2, OWN, COLS), jnp.float32),
            pltpu.VMEM((NQ, NYH * OWN, TOK), A_TYPE),
            pltpu.VMEM((NQ, NYH * OWN, TOK), A_TYPE),
            pltpu.VMEM((NY, NYH * OWN, TOK), jnp.float32),
            pltpu.VMEM((NX - 1, NYH * OWN, COLS), D_TYPE),
            pltpu.VMEM((NX - 1, NYH * OWN, COLS), D_TYPE),
            pltpu.VMEM((NYH * OWN, COLS), jnp.float32),
            pltpu.SemaphoreType.DMA((9,)),
            pltpu.SemaphoreType.DMA((2,)),
            pltpu.SemaphoreType.DMA((2, NQ)),
            pltpu.SemaphoreType.DMA((2, NY)),
            pltpu.SemaphoreType.DMA((2, NX)),
            pltpu.SemaphoreType.DMA((2, NZ)),
            pltpu.SemaphoreType.DMA((2, NZ)),
        ],
        compiler_params=pltpu.CompilerParams(
            collective_id=0, has_side_effects=True, vmem_limit_bytes=56 * 1024 * 1024
        ),
        name="directions",
    )(activations, out_grads, projector, weight, moment, second)
    return pl.pallas_call(
        finish,
        out_shape=(
            jax.ShapeDtypeStruct(weight.shape, jnp.bfloat16),
            jax.ShapeDtypeStruct(moment.shape, jnp.float32),
            jax.ShapeDtypeStruct(second.shape, jnp.float32),
        ),
        in_specs=[vmem] * 4,
        out_specs=[any_space] * 3,
        scratch_shapes=[pltpu.VMEM((256, COLS), jnp.bfloat16), pltpu.SemaphoreType.DMA((3,))],
        compiler_params=pltpu.CompilerParams(vmem_limit_bytes=4 * 1024 * 1024),
        name="finish",
    )(*held)


def solution(mesh):
    in_specs = (
        P("dp", "row"),
        P("dp", "col"),
        P("row", None),
        P("row", ("col", "dp")),
        P("row", ("col", "dp")),
        P("row", ("col", "dp")),
    )
    out_specs = (P("row", ("col", "dp")), P("row", ("col", "dp")), P("row", ("col", "dp")))
    return jax.shard_map(
        per_device, mesh=mesh, in_specs=in_specs, out_specs=out_specs, check_vma=False
    )
```

```python
import jax
import jax.numpy as jnp
from jax import lax
from jax.experimental import pallas as pl
from jax.experimental.pallas import tpu as pltpu
from jax.sharding import PartitionSpec as P

MESH = pl.DeviceIdType.MESH
A_TYPE = jnp.bfloat16
NEAR = (0, 1, 7)
D_TYPE = jnp.float32

NZ, NK, NYH, NYL, NX = 8, 2, 2, 4, 4
NQ, NY = NZ * NK, NYH * NYL
OWN = 8
TOK = 128
R = 256
COLS = 896
CHUNKS = (pl.ds(0, 512), pl.ds(512, 384))
FAR_FIRST = (4, 3, 5, 2, 6, 1, 7)
NEAR_FIRST = (1, 7, 2, 6, 3, 5, 4)
F_ORDER = FAR_FIRST
PASSED_ON = ((1, 2), (3, 2), (5, 2), (7, 1))
FIRST_FIX = 1.0 / (1.0 - 0.9**10)
SECOND_FIX = 1.0 / (1.0 - 0.999**10)


def kernel(
    act, grads, proj, weight, moment, second,
    out_v, state_v,
    act_v, proj_v, perm_v, weight_v, grads_v, mv, near_a, far_a, got_near_a, got_far_a, recv_b, send_d, recv_d, low_v, dirs,
    in_sem, mv_sem, a_sem, b_sem, d_sem, f_send, f_recv, c_send, c_recv,
):
    row, col, dp = lax.axis_index("row"), lax.axis_index("col"), lax.axis_index("dp")
    yh, z, k = row // NQ, (row // NK) % NZ, row % NK
    y, q = yh * NYL + col, row % NQ

    def at_zk(dz, dk):
        return (yh * NQ + ((z + dz) % NZ) * NK + (k + dk) % NK, col, dp)

    def at_y(dy):
        to = (y + dy) % NY
        return ((to // NYL) * NQ + q, to % NYL, dp)

    def at_x(dx):
        return (row, col, (dp + dx) % NX)

    zk = [(dz, dk) for dz in FAR_FIRST for dk in range(NK)] + [(0, 1)]

    loads = [
        pltpu.make_async_copy(act.at[pl.ds(pl.multiple_of(col * TOK, TOK), TOK), :], act_v, in_sem.at[0]),
        pltpu.make_async_copy(proj, proj_v, in_sem.at[1]),
        pltpu.make_async_copy(moment, mv.at[yh, 0], in_sem.at[2]),
        pltpu.make_async_copy(second, mv.at[yh, 1], in_sem.at[3]),
    ]
    for x in range(NX):
        loads.append(pltpu.make_async_copy(grads.at[:, pl.ds(x * COLS, COLS)], grads_v.at[x], in_sem.at[4 + x]))
    loads.append(pltpu.make_async_copy(weight, weight_v, in_sem.at[8]))
    barrier = pltpu.get_barrier_semaphore()
    peers = []
    for far in FAR_FIRST:
        peers += [at_zk(far, 1), at_zk(far, 0), at_y(far)] + ([at_x(far)] if far < NX else [])
    peers.append(at_zk(0, 1))
    for peer in peers:
        pl.semaphore_signal(barrier, inc=1, device_id=peer, device_id_type=MESH)
    for load in loads:
        load.start()

    loads[0].wait()
    loads[1].wait()
    part = lax.dot_general(proj_v[...], act_v[...], (((0,), (1,)), ((), ())), preferred_element_type=jnp.float32)
    part = part.reshape(NYH, NQ, OWN, TOK)
    part = jnp.concatenate([part[0], part[1]], axis=1)
    near_a[...] = part
    far_a[...] = part.astype(A_TYPE)

    pl.semaphore_wait(barrier, len(peers))

    sends_a = []
    for j, (dz, dk) in enumerate(zk):
        to = ((z + dz) % NZ) * NK + (k + dk) % NK
        sent, got = (near_a, got_near_a) if dz in NEAR else (far_a, got_far_a)
        copy = pltpu.make_async_remote_copy(
            src_ref=sent.at[to], dst_ref=got.at[j], send_sem=a_sem.at[0, j], recv_sem=a_sem.at[1, j],
            device_id=at_zk(dz, dk), device_id_type=MESH,
        )
        copy.start()
        sends_a.append((copy, got.at[j]))

    loads[2].wait()
    loads[3].wait()
    send_mv = pltpu.make_async_remote_copy(
        src_ref=mv.at[yh], dst_ref=mv.at[yh], send_sem=mv_sem.at[0], recv_sem=mv_sem.at[1],
        device_id=at_y(NYL), device_id_type=MESH,
    )
    send_mv.start()

    source = lax.broadcasted_iota(jnp.int32, (R, R), 0)
    place = lax.broadcasted_iota(jnp.int32, (R, R), 1)
    core, step, half, rank = place // (R // NK), place // (NYH * OWN) % NZ, place // OWN % NYH, place % OWN
    from_z = (z + NZ - jnp.where(step % 2 == 1, (step + 1) // 2, (NZ - step // 2) % NZ)) % NZ
    wanted = ((half * NZ + from_z) * NK + core) * OWN + rank
    shuffle = jnp.where(source == wanted, 1.0, 0.0).astype(jnp.bfloat16)
    perm_v[...] = jnp.dot(proj_v[...], shuffle, preferred_element_type=jnp.float32).astype(jnp.bfloat16)

    total = near_a[q]
    for copy, got in reversed(sends_a):
        copy.wait_recv()
        total += got[...].astype(jnp.float32)
    sends_a = [copy for copy, _ in sends_a]

    recv_b[y] = total
    sends_b = []
    for j, dy in enumerate(FAR_FIRST):
        copy = pltpu.make_async_remote_copy(
            src_ref=recv_b.at[y], dst_ref=recv_b.at[y], send_sem=b_sem.at[0, j], recv_sem=b_sem.at[1, j],
            device_id=at_y(dy), device_id_type=MESH,
        )
        copy.start()
        sends_b.append(copy)
    for load in loads[4:8]:
        load.wait()
    for copy in sends_b:
        copy.wait_recv()
    coords = jnp.concatenate([recv_b[c] + recv_b[NYL + c] for c in range(NYL)], axis=1)
    high = coords.astype(jnp.bfloat16)
    rest = (coords - high.astype(jnp.float32)).astype(jnp.bfloat16)
    both = jnp.concatenate([high, rest], axis=0)

    def low_of(to, at):
        product = jnp.dot(both, grads_v[to, :, at], preferred_element_type=jnp.float32)
        return product[: NYH * OWN] + product[NYH * OWN :]

    sends_d = []
    for c, at in enumerate(CHUNKS):
        for j, dx in enumerate((2, 1, 3)):
            send_d[j, :, at] = low_of((dp + dx) % NX, at).astype(D_TYPE)
            copy = pltpu.make_async_remote_copy(
                src_ref=send_d.at[j, :, at], dst_ref=recv_d.at[j, :, at],
                send_sem=d_sem.at[0, c, j], recv_sem=d_sem.at[1, c, j],
                device_id=at_x(dx), device_id_type=MESH,
            )
            copy.start()
            sends_d.append(copy)
    for at in CHUNKS:
        low_v[:, at] = low_of(dp, at)
    send_mv.wait_recv()

    def passed(to, source, target, send_sem, recv_sem):
        return pltpu.make_async_remote_copy(
            src_ref=source, dst_ref=target, send_sem=send_sem, recv_sem=recv_sem, device_id=to, device_id_type=MESH
        )

    def over_z(dz, j, c, at):
        return passed(
            at_zk(dz, 1 - k), dirs.at[k, 0, :, at], dirs.at[k, 1 + j, :, at], f_send.at[c, j], f_recv.at[c, j, k]
        )

    def over_core(g, c, at):
        here = dirs.at[:, pl.ds(*PASSED_ON[g]), :, at]
        return passed(at_zk(0, 1), here, here, c_send.at[c, 1 + g], c_recv.at[c, 1 + g])

    sends_f, sends_c = [], []
    for c, at in enumerate(CHUNKS):
        for copy in sends_d[c * (NX - 1) : (c + 1) * (NX - 1)]:
            copy.wait_recv()
        low = low_v[:, at]
        for j in (1, 2, 0):
            low += recv_d[j, :, at].astype(jnp.float32)
        low = (low * (1.0 / NX)).reshape(NYH, OWN, -1)
        state_m = 0.9 * mv[:, 0, :, at] + 0.1 * low
        state_s = 0.999 * mv[:, 1, :, at] + 0.001 * low * low
        direction = state_m * FIRST_FIX / (jnp.sqrt(state_s * SECOND_FIX) + 1e-08)
        dirs[k, 0, :, at] = direction.reshape(NYH * OWN, -1).astype(jnp.bfloat16)
        for dz in F_ORDER:
            sends_f.append(over_z(dz, NEAR_FIRST.index(dz), c, at))
            sends_f[-1].start()
        own = dirs.at[k, 0, :, at]
        sends_c.append(passed(at_zk(0, 1), own, own, c_send.at[c, 0], c_recv.at[c, 0]))
        sends_c[c].start()
        state_v[0, :, at] = jnp.where(yh == 0, state_m[0], state_m[1])
        state_v[1, :, at] = jnp.where(yh == 0, state_s[0], state_s[1])
    loads[8].wait()

    def update(at):
        product = jnp.dot(perm_v[...], dirs[:, :, :, at].reshape(R, -1), preferred_element_type=jnp.float32)
        out_v[:, at] = (weight_v[:, at].astype(jnp.float32) - 0.5 * product).astype(jnp.bfloat16)

    @pl.when(k == 1)
    def _():
        for c, at in enumerate(CHUNKS):
            for g, (first, count) in enumerate(PASSED_ON):
                for j in range(first - 1, first - 1 + count):
                    for core in range(NK):
                        ref = dirs.at[core, 1 + j, :, at]
                        passed(at_zk(0, 1), ref, ref, f_send.at[c, j], f_recv.at[c, j, core]).wait_recv()
                over_core(g, c, at).start()
        for c, at in enumerate(CHUNKS):
            sends_c[c].wait_recv()
            update(at)
        for c, at in enumerate(CHUNKS):
            for g in range(len(PASSED_ON)):
                over_core(g, c, at).wait_send()

    @pl.when(k == 0)
    def _():
        for c, at in enumerate(CHUNKS):
            sends_c[c].wait_recv()
            for g in range(len(PASSED_ON)):
                over_core(g, c, at).wait_recv()
            update(at)

    for copy in sends_a + [send_mv] + sends_b + sends_d + sends_f + sends_c:
        copy.wait_send()


def store(weight, state, new_weight, new_moment, new_second, out_sem):
    copies = [
        pltpu.make_async_copy(weight, new_weight, out_sem.at[0]),
        pltpu.make_async_copy(state.at[0], new_moment, out_sem.at[1]),
        pltpu.make_async_copy(state.at[1], new_second, out_sem.at[2]),
    ]
    for copy in copies:
        copy.start()
    for copy in copies:
        copy.wait()


def per_device(activations, out_grads, projector, weight, moment, second):
    any_space = pl.BlockSpec(memory_space=pl.ANY)
    vmem = pl.BlockSpec(memory_space=pltpu.VMEM)
    held = pl.pallas_call(
        kernel,
        out_shape=(
            pltpu.VMEM((256, COLS), jnp.bfloat16),
            pltpu.VMEM((2, OWN, COLS), jnp.float32),
        ),
        in_specs=[any_space] * 6,
        out_specs=[vmem] * 2,
        scratch_shapes=[
            pltpu.VMEM((TOK, 256), jnp.bfloat16),
            pltpu.VMEM((256, R), jnp.bfloat16),
            pltpu.VMEM((256, R), jnp.bfloat16),
            pltpu.VMEM((256, COLS), jnp.bfloat16),
            pltpu.VMEM((NX, 512, COLS), jnp.bfloat16),
            pltpu.VMEM((NYH, 2, OWN, COLS), jnp.float32),
            pltpu.VMEM((NQ, NYH * OWN, TOK), jnp.float32),
            pltpu.VMEM((NQ, NYH * OWN, TOK), A_TYPE),
            pltpu.VMEM((NQ, NYH * OWN, TOK), jnp.float32),
            pltpu.VMEM((NQ, NYH * OWN, TOK), A_TYPE),
            pltpu.VMEM((NY, NYH * OWN, TOK), jnp.float32),
            pltpu.VMEM((NX - 1, NYH * OWN, COLS), D_TYPE),
            pltpu.VMEM((NX - 1, NYH * OWN, COLS), D_TYPE),
            pltpu.VMEM((NYH * OWN, COLS), jnp.float32),
            pltpu.VMEM((NK, NZ, NYH * OWN, COLS), jnp.bfloat16),
            pltpu.SemaphoreType.DMA((9,)),
            pltpu.SemaphoreType.DMA((2,)),
            pltpu.SemaphoreType.DMA((2, NQ)),
            pltpu.SemaphoreType.DMA((2, NY)),
            pltpu.SemaphoreType.DMA((2, len(CHUNKS), NX)),
            pltpu.SemaphoreType.DMA((len(CHUNKS), NZ)),
            pltpu.SemaphoreType.DMA((len(CHUNKS), NZ, NK)),
            pltpu.SemaphoreType.DMA((len(CHUNKS), NZ)),
            pltpu.SemaphoreType.DMA((len(CHUNKS), NZ)),
        ],
        compiler_params=pltpu.CompilerParams(
            collective_id=0, has_side_effects=True, vmem_limit_bytes=56 * 1024 * 1024
        ),
        name="directions",
    )(activations, out_grads, projector, weight, moment, second)
    return pl.pallas_call(
        store,
        out_shape=(
            jax.ShapeDtypeStruct(weight.shape, jnp.bfloat16),
            jax.ShapeDtypeStruct(moment.shape, jnp.float32),
            jax.ShapeDtypeStruct(second.shape, jnp.float32),
        ),
        in_specs=[vmem] * 2,
        out_specs=[any_space] * 3,
        scratch_shapes=[pltpu.SemaphoreType.DMA((3,))],
        compiler_params=pltpu.CompilerParams(vmem_limit_bytes=4 * 1024 * 1024),
        name="store",
    )(*held)


def solution(mesh):
    in_specs = (
        P("dp", "row"),
        P("dp", "col"),
        P("row", None),
        P("row", ("col", "dp")),
        P("row", ("col", "dp")),
        P("row", ("col", "dp")),
    )
    out_specs = (P("row", ("col", "dp")), P("row", ("col", "dp")), P("row", ("col", "dp")))
    return jax.shard_map(
        per_device, mesh=mesh, in_specs=in_specs, out_specs=out_specs, check_vma=False
    )
```

```python
import jax
import jax.numpy as jnp
from jax import lax
from jax.experimental import pallas as pl
from jax.experimental.pallas import tpu as pltpu
from jax.sharding import PartitionSpec as P

MESH = pl.DeviceIdType.MESH
NZ, NK, NYH, NYL, NX = 8, 2, 2, 4, 4
NQ, NY = NZ * NK, NYH * NYL
OWN = 8
TOK = 128
R = 256
COLS = 896
CHUNKS = (pl.ds(0, 512), pl.ds(512, 384))
FAR_FIRST = (4, 3, 5, 2, 6, 1, 7)
FAR, NEAR = FAR_FIRST[:5], FAR_FIRST[5:]
GROUPS = ((1, 1), (2, 2), (4, 2), (6, 2))
FIRST_FIX = 1.0 / (1.0 - 0.9**10)
SECOND_FIX = 1.0 / (1.0 - 0.999**10)


def kernel(
    act, grads, proj, weight, moment, second,
    out_v, state_v,
    first_v, perm_v, weight_v, grads_v, mv, near_a, far_a, got_near_a, got_far_a, recv_b, send_d, recv_d, low_v, dirs,
    first_sem, mv_in_sem, grads_sem, weight_sem, mv_sem, near_sem, far_sem, b_sem, d_send, d_recv, f_send, f_recv,
    own_send, own_recv, pass_send, pass_recv,
):
    row, col, dp = lax.axis_index("row"), lax.axis_index("col"), lax.axis_index("dp")
    yh, z, k = row // NQ, (row // NK) % NZ, row % NK
    y, q = yh * NYL + col, row % NQ

    def at_zk(dz, dk):
        return (yh * NQ + ((z + dz) % NZ) * NK + (k + dk) % NK, col, dp)

    def at_y(dy):
        to = (y + dy) % NY
        return ((to // NYL) * NQ + q, to % NYL, dp)

    def at_x(dx):
        return (row, col, (dp + dx) % NX)

    def send(source, target, send_sem, recv_sem, to):
        copy = pltpu.make_async_remote_copy(
            src_ref=source, dst_ref=target, send_sem=send_sem, recv_sem=recv_sem, device_id=to, device_id_type=MESH
        )
        copy.start()

    def wait(ref, sem):
        pltpu.make_async_copy(ref, ref, sem).wait()

    barrier = pltpu.get_barrier_semaphore()
    peers = []
    for far in FAR_FIRST:
        peers += [at_zk(far, 1), at_zk(far, 0), at_y(far)] + ([at_x(far)] if far < NX else [])
    peers.append(at_zk(0, 1))
    for peer in peers:
        pl.semaphore_signal(barrier, inc=1, device_id=peer, device_id_type=MESH)

    tokens = pl.ds(pl.multiple_of(col * TOK, TOK), TOK)
    pltpu.make_async_copy(act.at[tokens, :], first_v.at[pl.ds(0, TOK), :], first_sem).start()
    pltpu.make_async_copy(proj, first_v.at[pl.ds(TOK, R), :], first_sem).start()
    pltpu.make_async_copy(moment, mv.at[yh, 0], mv_in_sem).start()
    pltpu.make_async_copy(second, mv.at[yh, 1], mv_in_sem).start()
    for x in range(NX):
        pltpu.make_async_copy(grads.at[:, pl.ds(x * COLS, COLS)], grads_v.at[x], grads_sem).start()
    pltpu.make_async_copy(weight, weight_v, weight_sem).start()

    wait(first_v, first_sem)
    block = first_v[TOK:]
    part = lax.dot_general(block, first_v[:TOK], (((0,), (1,)), ((), ())), preferred_element_type=jnp.float32)
    part = part.reshape(NYH, NQ, OWN, TOK)
    part = jnp.concatenate([part[0], part[1]], axis=1)
    near_a[...] = part
    far_a[...] = part.astype(jnp.bfloat16)

    pl.semaphore_wait(barrier, len(peers))

    for i, (dz, dk) in enumerate([(dz, dk) for dz in FAR for dk in range(NK)]):
        to = ((z + dz) % NZ) * NK + (k + dk) % NK
        send(far_a.at[to], got_far_a.at[i], far_sem.at[0], far_sem.at[1], at_zk(dz, dk))
    for i, (dz, dk) in enumerate([(dz, dk) for dz in NEAR for dk in range(NK)] + [(0, 1)]):
        to = ((z + dz) % NZ) * NK + (k + dk) % NK
        send(near_a.at[to], got_near_a.at[i], near_sem.at[0], near_sem.at[1], at_zk(dz, dk))

    source = lax.broadcasted_iota(jnp.int32, (R, R), 0)
    place = lax.broadcasted_iota(jnp.int32, (R, R), 1)
    step, core, half, rank = place // (R // NZ), place // (NYH * OWN) % NK, place // OWN % NYH, place % OWN
    from_z = (z + NZ - jnp.where(step % 2 == 1, (step + 1) // 2, (NZ - step // 2) % NZ)) % NZ
    wanted = ((half * NZ + from_z) * NK + core) * OWN + rank
    shuffle = jnp.where(source == wanted, 1.0, 0.0).astype(jnp.bfloat16)
    perm_v[...] = jnp.dot(block, shuffle, preferred_element_type=jnp.float32).astype(jnp.bfloat16)

    wait(got_near_a, near_sem.at[1])
    total = near_a[q] + jnp.sum(got_near_a[...], axis=0)
    wait(got_far_a, far_sem.at[1])
    total += jnp.sum(got_far_a[...].astype(jnp.float32), axis=0)

    recv_b[y] = total
    for dy in FAR_FIRST:
        send(recv_b.at[y], recv_b.at[y], b_sem.at[0], b_sem.at[1], at_y(dy))

    wait(mv.at[yh], mv_in_sem)
    send(mv.at[yh], mv.at[yh], mv_sem.at[0], mv_sem.at[1], at_y(NYL))

    wait(grads_v, grads_sem)
    wait(recv_b.at[pl.ds(0, NY - 1)], b_sem.at[1])
    coords = jnp.concatenate([recv_b[c] + recv_b[NYL + c] for c in range(NYL)], axis=1)
    high = coords.astype(jnp.bfloat16)
    rest = (coords - high.astype(jnp.float32)).astype(jnp.bfloat16)
    both = jnp.concatenate([high, rest], axis=0)

    def low_of(to, at):
        product = jnp.dot(both, grads_v[to, :, at], preferred_element_type=jnp.float32)
        return product[: NYH * OWN] + product[NYH * OWN :]

    for c, at in enumerate(CHUNKS):
        for j, dx in enumerate((2, 1, 3)):
            send_d[j, :, at] = low_of((dp + dx) % NX, at)
            send(send_d.at[j, :, at], recv_d.at[j, :, at], d_send, d_recv.at[c], at_x(dx))
    for at in CHUNKS:
        low_v[:, at] = low_of(dp, at)
    wait(mv.at[yh], mv_sem.at[1])

    for c, at in enumerate(CHUNKS):
        wait(recv_d.at[:, :, at], d_recv.at[c])
        low = low_v[:, at] + recv_d[1, :, at] + recv_d[2, :, at] + recv_d[0, :, at]
        low = (low * (1.0 / NX)).reshape(NYH, OWN, -1)
        state_m = 0.9 * mv[:, 0, :, at] + 0.1 * low
        state_s = 0.999 * mv[:, 1, :, at] + 0.001 * low * low
        direction = state_m * FIRST_FIX / (jnp.sqrt(state_s * SECOND_FIX) + 1e-08)
        dirs[0, k, :, at] = direction.reshape(NYH * OWN, -1).astype(jnp.bfloat16)
        own = dirs.at[0, k, :, at]
        for i in range(NZ - 1):
            dz = (i + (i - z + NZ) // NZ - z + NZ) % NZ
            back = dz // (NZ // 2 + 1)
            slot = (2 * dz - 1) * (1 - back) + (2 * NZ - 2 * dz) * back
            send(own, dirs.at[slot, k, :, at], f_send, f_recv.at[c, slot // 2], at_zk(dz, 1 - k))
        send(own, own, own_send, own_recv.at[c], at_zk(0, 1))
        state_v[0, :, at] = jnp.where(yh == 0, state_m[0], state_m[1])
        state_v[1, :, at] = jnp.where(yh == 0, state_s[0], state_s[1])
    wait(weight_v, weight_sem)

    def update(at):
        product = jnp.dot(perm_v[...], dirs[:, :, :, at].reshape(R, -1), preferred_element_type=jnp.float32)
        out_v[:, at] = (weight_v[:, at].astype(jnp.float32) - 0.5 * product).astype(jnp.bfloat16)

    @pl.when(k == 1)
    def _():
        for c, at in enumerate(CHUNKS):
            for g, (first, count) in enumerate(GROUPS):
                here = dirs.at[pl.ds(first, count), :, :, at]
                wait(here, f_recv.at[c, g])
                send(here, here, pass_send, pass_recv.at[c], at_zk(0, 1))
        for c, at in enumerate(CHUNKS):
            wait(dirs.at[0, 0, :, at], own_recv.at[c])
            update(at)
        wait(dirs.at[pl.ds(1, NZ - 1)], pass_send)

    @pl.when(k == 0)
    def _():
        for c, at in enumerate(CHUNKS):
            wait(dirs.at[0, 0, :, at], own_recv.at[c])
            wait(dirs.at[pl.ds(1, NZ - 1), :, :, at], pass_recv.at[c])
            update(at)

    wait(far_a.at[pl.ds(0, len(FAR) * NK)], far_sem.at[0])
    wait(near_a.at[pl.ds(0, len(NEAR) * NK + 1)], near_sem.at[0])
    wait(mv.at[0], mv_sem.at[0])
    wait(recv_b.at[pl.ds(0, NY - 1)], b_sem.at[0])
    wait(send_d, d_send)
    wait(dirs.at[pl.ds(0, NZ - 1), 0], f_send)
    wait(dirs.at[0, 0], own_send)


def store(weight, state, new_weight, new_moment, new_second, out_sem):
    copies = [
        pltpu.make_async_copy(weight, new_weight, out_sem.at[0]),
        pltpu.make_async_copy(state.at[0], new_moment, out_sem.at[1]),
        pltpu.make_async_copy(state.at[1], new_second, out_sem.at[2]),
    ]
    for copy in copies:
        copy.start()
    for copy in copies:
        copy.wait()


def per_device(activations, out_grads, projector, weight, moment, second):
    any_space = pl.BlockSpec(memory_space=pl.ANY)
    vmem = pl.BlockSpec(memory_space=pltpu.VMEM)
    held = pl.pallas_call(
        kernel,
        out_shape=(
            pltpu.VMEM((256, COLS), jnp.bfloat16),
            pltpu.VMEM((2, OWN, COLS), jnp.float32),
        ),
        in_specs=[any_space] * 6,
        out_specs=[vmem] * 2,
        scratch_shapes=[
            pltpu.VMEM((TOK + R, R), jnp.bfloat16),
            pltpu.VMEM((256, R), jnp.bfloat16),
            pltpu.VMEM((256, COLS), jnp.bfloat16),
            pltpu.VMEM((NX, 512, COLS), jnp.bfloat16),
            pltpu.VMEM((NYH, 2, OWN, COLS), jnp.float32),
            pltpu.VMEM((NQ, NYH * OWN, TOK), jnp.float32),
            pltpu.VMEM((NQ, NYH * OWN, TOK), jnp.bfloat16),
            pltpu.VMEM((len(NEAR) * NK + 1, NYH * OWN, TOK), jnp.float32),
            pltpu.VMEM((len(FAR) * NK, NYH * OWN, TOK), jnp.bfloat16),
            pltpu.VMEM((NY, NYH * OWN, TOK), jnp.float32),
            pltpu.VMEM((NX - 1, NYH * OWN, COLS), jnp.float32),
            pltpu.VMEM((NX - 1, NYH * OWN, COLS), jnp.float32),
            pltpu.VMEM((NYH * OWN, COLS), jnp.float32),
            pltpu.VMEM((NZ, NK, NYH * OWN, COLS), jnp.bfloat16),
            *[pltpu.SemaphoreType.DMA(())] * 4,
            *[pltpu.SemaphoreType.DMA((2,))] * 4,
            pltpu.SemaphoreType.DMA(()),
            pltpu.SemaphoreType.DMA((len(CHUNKS),)),
            pltpu.SemaphoreType.DMA(()),
            pltpu.SemaphoreType.DMA((len(CHUNKS), len(GROUPS))),
            pltpu.SemaphoreType.DMA(()),
            pltpu.SemaphoreType.DMA((len(CHUNKS),)),
            pltpu.SemaphoreType.DMA(()),
            pltpu.SemaphoreType.DMA((len(CHUNKS),)),
        ],
        compiler_params=pltpu.CompilerParams(
            collective_id=0, has_side_effects=True, vmem_limit_bytes=56 * 1024 * 1024
        ),
        name="directions",
    )(activations, out_grads, projector, weight, moment, second)
    return pl.pallas_call(
        store,
        out_shape=(
            jax.ShapeDtypeStruct(weight.shape, jnp.bfloat16),
            jax.ShapeDtypeStruct(moment.shape, jnp.float32),
            jax.ShapeDtypeStruct(second.shape, jnp.float32),
        ),
        in_specs=[vmem] * 2,
        out_specs=[any_space] * 3,
        scratch_shapes=[pltpu.SemaphoreType.DMA((3,))],
        compiler_params=pltpu.CompilerParams(vmem_limit_bytes=4 * 1024 * 1024),
        name="store",
    )(*held)


def solution(mesh):
    in_specs = (
        P("dp", "row"),
        P("dp", "col"),
        P("row", None),
        P("row", ("col", "dp")),
        P("row", ("col", "dp")),
        P("row", ("col", "dp")),
    )
    out_specs = (P("row", ("col", "dp")), P("row", ("col", "dp")), P("row", ("col", "dp")))
    return jax.shard_map(
        per_device, mesh=mesh, in_specs=in_specs, out_specs=out_specs, check_vma=False
    )
```

```python
import jax
import jax.numpy as jnp
from jax import lax
from jax.experimental import pallas as pl
from jax.experimental.pallas import tpu as pltpu
from jax.sharding import PartitionSpec as P

MESH = pl.DeviceIdType.MESH
NZ, NK, NYH, NYL, NX = 8, 2, 2, 4, 4
NQ, NY = NZ * NK, NYH * NYL
OWN = 8
TOK = 128
R = 256
COLS = 896
CHUNKS = (pl.ds(0, 512), pl.ds(512, 384))
FAR_FIRST = (4, 3, 5, 2, 6, 1, 7)
FAR, NEAR = FAR_FIRST[:5], FAR_FIRST[5:]
EARLY = 2
GROUPS = ((1, 1), (2, 2), (4, 2), (6, 2))
FIRST_FIX = 1.0 / (1.0 - 0.9**10)
SECOND_FIX = 1.0 / (1.0 - 0.999**10)


def other(i, me, n):
    return (i + (i - me + n) // n - me + n) % n


def kernel(
    act, grads, proj, weight, moment, second,
    out_v, state_v,
    first_v, perm_v, weight_v, grads_v, mv, near_a, far_a, got_near_a, got_far_a, recv_b, send_d, recv_d, low_v, dirs,
    first_sem, mv_in_sem, grads_sem, weight_sem, mv_sem, near_sem, far_sem, b_sem, d_send, d_recv, f_send, f_recv,
    own_send, own_recv, pass_send, pass_recv,
):
    row, col, dp = lax.axis_index("row"), lax.axis_index("col"), lax.axis_index("dp")
    yh, z, k = row // NQ, (row // NK) % NZ, row % NK
    y, q = yh * NYL + col, row % NQ

    def at_zk(dz, dk):
        return (yh * NQ + ((z + dz) % NZ) * NK + (k + dk) % NK, col, dp)

    def at_y(dy):
        to = (y + dy) % NY
        return ((to // NYL) * NQ + q, to % NYL, dp)

    def at_x(dx):
        return (row, col, (dp + dx) % NX)

    def send(source, target, send_sem, recv_sem, to):
        copy = pltpu.make_async_remote_copy(
            src_ref=source, dst_ref=target, send_sem=send_sem, recv_sem=recv_sem, device_id=to, device_id_type=MESH
        )
        copy.start()

    def wait(ref, sem):
        pltpu.make_async_copy(ref, ref, sem).wait()

    barrier = pltpu.get_barrier_semaphore()
    peers = []
    for far in FAR_FIRST:
        peers += [at_zk(far, 1), at_zk(far, 0), at_y(far)] + ([at_x(far)] if far < NX else [])
    peers.append(at_zk(0, 1))
    for peer in peers:
        pl.semaphore_signal(barrier, inc=1, device_id=peer, device_id_type=MESH)

    tokens = pl.ds(pl.multiple_of(col * TOK, TOK), TOK)
    pltpu.make_async_copy(act.at[tokens, :], first_v.at[pl.ds(0, TOK), :], first_sem).start()
    pltpu.make_async_copy(proj, first_v.at[pl.ds(TOK, R), :], first_sem).start()
    pltpu.make_async_copy(moment, mv.at[yh, 0], mv_in_sem).start()
    pltpu.make_async_copy(second, mv.at[yh, 1], mv_in_sem).start()
    for x in range(NX):
        pltpu.make_async_copy(grads.at[:, pl.ds(x * COLS, COLS)], grads_v.at[x], grads_sem).start()
    pltpu.make_async_copy(weight, weight_v, weight_sem).start()

    wait(first_v, first_sem)
    block = first_v[TOK:]
    part = lax.dot_general(block, first_v[:TOK], (((0,), (1,)), ((), ())), preferred_element_type=jnp.float32)
    part = part.reshape(NYH, NQ, OWN, TOK)
    part = jnp.concatenate([part[0], part[1]], axis=1)
    near_a[...] = part
    far_a[...] = part.astype(jnp.bfloat16)

    pl.semaphore_wait(barrier, len(peers))

    for i, (dz, dk) in enumerate([(dz, dk) for dz in FAR for dk in range(NK)]):
        to = ((z + dz) % NZ) * NK + (k + dk) % NK
        send(far_a.at[to], got_far_a.at[i], far_sem.at[0], far_sem.at[1], at_zk(dz, dk))
    for i, (dz, dk) in enumerate([(dz, dk) for dz in NEAR for dk in range(NK)] + [(0, 1)]):
        to = ((z + dz) % NZ) * NK + (k + dk) % NK
        send(near_a.at[to], got_near_a.at[i], near_sem.at[0], near_sem.at[1], at_zk(dz, dk))

    source = lax.broadcasted_iota(jnp.int32, (R, R), 0)
    place = lax.broadcasted_iota(jnp.int32, (R, R), 1)
    step, core, half, rank = place // (R // NZ), place // (NYH * OWN) % NK, place // OWN % NYH, place % OWN
    from_z = (z + NZ - jnp.where(step % 2 == 1, (step + 1) // 2, (NZ - step // 2) % NZ)) % NZ
    wanted = ((half * NZ + from_z) * NK + core) * OWN + rank
    shuffle = jnp.where(source == wanted, 1.0, 0.0).astype(jnp.bfloat16)
    perm_v[...] = jnp.dot(block, shuffle, preferred_element_type=jnp.float32).astype(jnp.bfloat16)

    wait(got_near_a, near_sem.at[1])
    total = near_a[q] + jnp.sum(got_near_a[...], axis=0)
    wait(got_far_a, far_sem.at[1])
    total += jnp.sum(got_far_a[...].astype(jnp.float32), axis=0)

    recv_b[y] = total
    for dy in [other(i, y, NY) for i in range(NY - 1)]:
        send(recv_b.at[y], recv_b.at[y], b_sem.at[0], b_sem.at[1], at_y(dy))

    wait(mv.at[yh], mv_in_sem)
    send(mv.at[yh], mv.at[yh], mv_sem.at[0], mv_sem.at[1], at_y(NYL))

    wait(grads_v, grads_sem)
    wait(recv_b.at[pl.ds(0, NY - 1)], b_sem.at[1])
    coords = jnp.concatenate([recv_b[c] + recv_b[NYL + c] for c in range(NYL)], axis=1)
    high = coords.astype(jnp.bfloat16)
    rest = (coords - high.astype(jnp.float32)).astype(jnp.bfloat16)
    both = jnp.concatenate([high, rest], axis=0)

    def low_of(to, at):
        product = jnp.dot(both, grads_v[to, :, at], preferred_element_type=jnp.float32)
        return product[: NYH * OWN] + product[NYH * OWN :]

    for c, at in enumerate(CHUNKS):
        for j in range(NX - 1):
            dx = other(j, dp, NX)
            send_d[j, :, at] = low_of((dp + dx) % NX, at)
            send(send_d.at[j, :, at], recv_d.at[dx - 1, :, at], d_send, d_recv.at[c], at_x(dx))
    for at in CHUNKS:
        low_v[:, at] = low_of(dp, at)
    wait(mv.at[yh], mv_sem.at[1])

    def over_z(c, at, i):
        dz = other(i, z, NZ)
        back = dz // (NZ // 2 + 1)
        slot = (2 * dz - 1) * (1 - back) + (2 * NZ - 2 * dz) * back
        send(dirs.at[0, k, :, at], dirs.at[slot, k, :, at], f_send, f_recv.at[c, slot // 2], at_zk(dz, 1 - k))

    for c, at in enumerate(CHUNKS):
        wait(recv_d.at[:, :, at], d_recv.at[c])
        low = low_v[:, at] + recv_d[0, :, at] + recv_d[1, :, at] + recv_d[2, :, at]
        low = (low * (1.0 / NX)).reshape(NYH, OWN, -1)
        state_m = 0.9 * mv[:, 0, :, at] + 0.1 * low
        state_s = 0.999 * mv[:, 1, :, at] + 0.001 * low * low
        direction = state_m * FIRST_FIX / (jnp.sqrt(state_s * SECOND_FIX) + 1e-08)
        dirs[0, k, :, at] = direction.reshape(NYH * OWN, -1).astype(jnp.bfloat16)
        for i in range(EARLY):
            over_z(c, at, i)
        own = dirs.at[0, k, :, at]
        send(own, own, own_send, own_recv.at[c], at_zk(0, 1))
        state_v[0, :, at] = jnp.where(yh == 0, state_m[0], state_m[1])
        state_v[1, :, at] = jnp.where(yh == 0, state_s[0], state_s[1])
    for c, at in enumerate(CHUNKS):
        for i in range(EARLY, NZ - 1):
            over_z(c, at, i)
    wait(weight_v, weight_sem)

    def update(at):
        product = jnp.dot(perm_v[...], dirs[:, :, :, at].reshape(R, -1), preferred_element_type=jnp.float32)
        out_v[:, at] = (weight_v[:, at].astype(jnp.float32) - 0.5 * product).astype(jnp.bfloat16)

    @pl.when(k == 1)
    def _():
        for c, at in enumerate(CHUNKS):
            for g, (first, count) in enumerate(GROUPS):
                here = dirs.at[pl.ds(first, count), :, :, at]
                wait(here, f_recv.at[c, g])
                send(here, here, pass_send, pass_recv.at[c], at_zk(0, 1))
            wait(dirs.at[0, 0, :, at], own_recv.at[c])
            update(at)
        wait(dirs.at[pl.ds(1, NZ - 1)], pass_send)

    @pl.when(k == 0)
    def _():
        for c, at in enumerate(CHUNKS):
            wait(dirs.at[0, 0, :, at], own_recv.at[c])
            wait(dirs.at[pl.ds(1, NZ - 1), :, :, at], pass_recv.at[c])
            update(at)

    wait(far_a.at[pl.ds(0, len(FAR) * NK)], far_sem.at[0])
    wait(near_a.at[pl.ds(0, len(NEAR) * NK + 1)], near_sem.at[0])
    wait(mv.at[0], mv_sem.at[0])
    wait(recv_b.at[pl.ds(0, NY - 1)], b_sem.at[0])
    wait(send_d, d_send)
    wait(dirs.at[pl.ds(0, NZ - 1), 0], f_send)
    wait(dirs.at[0, 0], own_send)


def store(weight, state, new_weight, new_moment, new_second, out_sem):
    copies = [
        pltpu.make_async_copy(weight, new_weight, out_sem.at[0]),
        pltpu.make_async_copy(state.at[0], new_moment, out_sem.at[1]),
        pltpu.make_async_copy(state.at[1], new_second, out_sem.at[2]),
    ]
    for copy in copies:
        copy.start()
    for copy in copies:
        copy.wait()


def per_device(activations, out_grads, projector, weight, moment, second):
    any_space = pl.BlockSpec(memory_space=pl.ANY)
    vmem = pl.BlockSpec(memory_space=pltpu.VMEM)
    held = pl.pallas_call(
        kernel,
        out_shape=(
            pltpu.VMEM((256, COLS), jnp.bfloat16),
            pltpu.VMEM((2, OWN, COLS), jnp.float32),
        ),
        in_specs=[any_space] * 6,
        out_specs=[vmem] * 2,
        scratch_shapes=[
            pltpu.VMEM((TOK + R, R), jnp.bfloat16),
            pltpu.VMEM((256, R), jnp.bfloat16),
            pltpu.VMEM((256, COLS), jnp.bfloat16),
            pltpu.VMEM((NX, 512, COLS), jnp.bfloat16),
            pltpu.VMEM((NYH, 2, OWN, COLS), jnp.float32),
            pltpu.VMEM((NQ, NYH * OWN, TOK), jnp.float32),
            pltpu.VMEM((NQ, NYH * OWN, TOK), jnp.bfloat16),
            pltpu.VMEM((len(NEAR) * NK + 1, NYH * OWN, TOK), jnp.float32),
            pltpu.VMEM((len(FAR) * NK, NYH * OWN, TOK), jnp.bfloat16),
            pltpu.VMEM((NY, NYH * OWN, TOK), jnp.float32),
            pltpu.VMEM((NX - 1, NYH * OWN, COLS), jnp.float32),
            pltpu.VMEM((NX - 1, NYH * OWN, COLS), jnp.float32),
            pltpu.VMEM((NYH * OWN, COLS), jnp.float32),
            pltpu.VMEM((NZ, NK, NYH * OWN, COLS), jnp.bfloat16),
            *[pltpu.SemaphoreType.DMA(())] * 4,
            *[pltpu.SemaphoreType.DMA((2,))] * 4,
            pltpu.SemaphoreType.DMA(()),
            pltpu.SemaphoreType.DMA((len(CHUNKS),)),
            pltpu.SemaphoreType.DMA(()),
            pltpu.SemaphoreType.DMA((len(CHUNKS), len(GROUPS))),
            pltpu.SemaphoreType.DMA(()),
            pltpu.SemaphoreType.DMA((len(CHUNKS),)),
            pltpu.SemaphoreType.DMA(()),
            pltpu.SemaphoreType.DMA((len(CHUNKS),)),
        ],
        compiler_params=pltpu.CompilerParams(
            collective_id=0, has_side_effects=True, vmem_limit_bytes=56 * 1024 * 1024
        ),
        name="directions",
    )(activations, out_grads, projector, weight, moment, second)
    return pl.pallas_call(
        store,
        out_shape=(
            jax.ShapeDtypeStruct(weight.shape, jnp.bfloat16),
            jax.ShapeDtypeStruct(moment.shape, jnp.float32),
            jax.ShapeDtypeStruct(second.shape, jnp.float32),
        ),
        in_specs=[vmem] * 2,
        out_specs=[any_space] * 3,
        scratch_shapes=[pltpu.SemaphoreType.DMA((3,))],
        compiler_params=pltpu.CompilerParams(vmem_limit_bytes=4 * 1024 * 1024),
        name="store",
    )(*held)


def solution(mesh):
    in_specs = (
        P("dp", "row"),
        P("dp", "col"),
        P("row", None),
        P("row", ("col", "dp")),
        P("row", ("col", "dp")),
        P("row", ("col", "dp")),
    )
    out_specs = (P("row", ("col", "dp")), P("row", ("col", "dp")), P("row", ("col", "dp")))
    return jax.shard_map(
        per_device, mesh=mesh, in_specs=in_specs, out_specs=out_specs, check_vma=False
    )
```

```python
import jax
import jax.numpy as jnp
from jax import lax
from jax.experimental import pallas as pl
from jax.experimental.pallas import tpu as pltpu
from jax.sharding import PartitionSpec as P

MESH = pl.DeviceIdType.MESH
NZ, NK, NYH, NYL, NX = 8, 2, 2, 4, 4
NQ, NY = NZ * NK, NYH * NYL
OWN = 8
TOK = 128
R = 256
COLS = 896
CHUNKS = (pl.ds(0, 512), pl.ds(512, 384))
FAR_FIRST = (4, 3, 5, 2, 6, 1, 7)
FAR, NEAR = FAR_FIRST[:5], FAR_FIRST[5:]
EARLY = 2
GROUPS = ((1, 1), (2, 2), (4, 2), (6, 2))
FIRST_FIX = 1.0 / (1.0 - 0.9**10)
SECOND_FIX = 1.0 / (1.0 - 0.999**10)


def other(i, me, n):
    return (i + (i - me + n) // n - me + n) % n


def kernel(
    act, grads, proj, weight, moment, second,
    out_v, state_v,
    first_v, perm_v, weight_v, grads_v, mv, near_a, far_a, got_near_a, got_far_a, recv_b, send_d, recv_d, low_v, dirs,
    first_sem, mv_in_sem, grads_sem, weight_sem, mv_sem, near_sem, far_sem, b_sem, d_send, d_recv, f_send, f_recv,
    own_send, own_recv, pass_send, pass_recv,
):
    row, col, dp = lax.axis_index("row"), lax.axis_index("col"), lax.axis_index("dp")
    yh, z, k = row // NQ, (row // NK) % NZ, row % NK
    y, q = yh * NYL + col, row % NQ

    def at_zk(dz, dk):
        return (yh * NQ + ((z + dz) % NZ) * NK + (k + dk) % NK, col, dp)

    def at_y(dy):
        to = (y + dy) % NY
        return ((to // NYL) * NQ + q, to % NYL, dp)

    def at_x(dx):
        return (row, col, (dp + dx) % NX)

    def send(source, target, send_sem, recv_sem, to):
        copy = pltpu.make_async_remote_copy(
            src_ref=source, dst_ref=target, send_sem=send_sem, recv_sem=recv_sem, device_id=to, device_id_type=MESH
        )
        copy.start()

    def wait(ref, sem):
        pltpu.make_async_copy(ref, ref, sem).wait()

    barrier = pltpu.get_barrier_semaphore()
    peers = []
    for far in FAR_FIRST:
        peers += [at_zk(far, 1), at_zk(far, 0), at_y(far)] + ([at_x(far)] if far < NX else [])
    peers.append(at_zk(0, 1))
    for peer in peers:
        pl.semaphore_signal(barrier, inc=1, device_id=peer, device_id_type=MESH)

    tokens = pl.ds(pl.multiple_of(col * TOK, TOK), TOK)
    pltpu.make_async_copy(act.at[tokens, :], first_v.at[pl.ds(0, TOK), :], first_sem).start()
    pltpu.make_async_copy(proj, first_v.at[pl.ds(TOK, R), :], first_sem).start()
    pltpu.make_async_copy(moment, mv.at[yh, 0], mv_in_sem).start()
    pltpu.make_async_copy(second, mv.at[yh, 1], mv_in_sem).start()
    for x in range(NX):
        pltpu.make_async_copy(grads.at[:, pl.ds(x * COLS, COLS)], grads_v.at[x], grads_sem).start()
    pltpu.make_async_copy(weight, weight_v, weight_sem).start()

    wait(first_v, first_sem)
    block = first_v[TOK:]
    part = lax.dot_general(block, first_v[:TOK], (((0,), (1,)), ((), ())), preferred_element_type=jnp.float32)
    part = part.reshape(NYH, NQ, OWN, TOK)
    part = jnp.concatenate([part[0], part[1]], axis=1)
    near_a[...] = part
    far_a[...] = part.astype(jnp.bfloat16)

    pl.semaphore_wait(barrier, len(peers))

    for i, (dz, dk) in enumerate([(dz, dk) for dz in FAR for dk in range(NK)]):
        to = ((z + dz) % NZ) * NK + (k + dk) % NK
        send(far_a.at[to], got_far_a.at[i], far_sem.at[0], far_sem.at[1], at_zk(dz, dk))
    for i, (dz, dk) in enumerate([(dz, dk) for dz in NEAR for dk in range(NK)] + [(0, 1)]):
        to = ((z + dz) % NZ) * NK + (k + dk) % NK
        send(near_a.at[to], got_near_a.at[i], near_sem.at[0], near_sem.at[1], at_zk(dz, dk))

    source = lax.broadcasted_iota(jnp.int32, (R, R), 0)
    place = lax.broadcasted_iota(jnp.int32, (R, R), 1)
    step, core, half, rank = place // (R // NZ), place // (NYH * OWN) % NK, place // OWN % NYH, place % OWN
    from_z = (z + NZ - jnp.where(step % 2 == 1, (step + 1) // 2, (NZ - step // 2) % NZ)) % NZ
    wanted = ((half * NZ + from_z) * NK + core) * OWN + rank
    shuffle = jnp.where(source == wanted, 1.0, 0.0).astype(jnp.bfloat16)
    perm_v[...] = jnp.dot(block, shuffle, preferred_element_type=jnp.float32).astype(jnp.bfloat16)

    wait(got_near_a, near_sem.at[1])
    total = near_a[q] + jnp.sum(got_near_a[...], axis=0)
    wait(got_far_a, far_sem.at[1])
    total += jnp.sum(got_far_a[...].astype(jnp.float32), axis=0)

    recv_b[y] = total
    for dy in [other(i, y, NY) for i in range(NY - 1)]:
        send(recv_b.at[y], recv_b.at[y], b_sem.at[0], b_sem.at[1], at_y(dy))

    wait(mv.at[yh], mv_in_sem)
    send(mv.at[yh], mv.at[yh], mv_sem.at[0], mv_sem.at[1], at_y(NYL))

    wait(grads_v, grads_sem)
    wait(recv_b.at[pl.ds(0, NY - 1)], b_sem.at[1])
    coords = jnp.concatenate([recv_b[c] + recv_b[NYL + c] for c in range(NYL)], axis=1)
    high = coords.astype(jnp.bfloat16)
    rest = (coords - high.astype(jnp.float32)).astype(jnp.bfloat16)
    both = jnp.concatenate([high, rest], axis=0)

    def low_of(to, at):
        product = jnp.dot(both, grads_v[to, :, at], preferred_element_type=jnp.float32)
        return product[: NYH * OWN] + product[NYH * OWN :]

    for c, at in enumerate(CHUNKS):
        for j in range(NX - 1):
            dx = other(j, dp, NX)
            send_d[j, :, at] = low_of((dp + dx) % NX, at)
            send(send_d.at[j, :, at], recv_d.at[dx - 1, :, at], d_send, d_recv.at[c], at_x(dx))
    for at in CHUNKS:
        low_v[:, at] = low_of(dp, at)
    wait(mv.at[yh], mv_sem.at[1])

    def over_z(c, at, i):
        dz = other(i, z, NZ)
        back = dz // (NZ // 2 + 1)
        slot = (2 * dz - 1) * (1 - back) + (2 * NZ - 2 * dz) * back
        send(dirs.at[0, k, :, at], dirs.at[slot, k, :, at], f_send, f_recv.at[c, slot // 2], at_zk(dz, 1 - k))

    for c, at in enumerate(CHUNKS):
        wait(recv_d.at[:, :, at], d_recv.at[c])
        low = low_v[:, at] + recv_d[0, :, at] + recv_d[1, :, at] + recv_d[2, :, at]
        low = (low * (1.0 / NX)).reshape(NYH, OWN, -1)
        state_m = 0.9 * mv[:, 0, :, at] + 0.1 * low
        state_s = 0.999 * mv[:, 1, :, at] + 0.001 * low * low
        direction = state_m * FIRST_FIX / (jnp.sqrt(state_s * SECOND_FIX) + 1e-08)
        dirs[0, k, :, at] = direction.reshape(NYH * OWN, -1).astype(jnp.bfloat16)
        own = dirs.at[0, k, :, at]
        send(own, own, own_send, own_recv.at[c], at_zk(0, 1))
        for i in range(EARLY):
            over_z(c, at, i)
        state_v[0, :, at] = jnp.where(yh == 0, state_m[0], state_m[1])
        state_v[1, :, at] = jnp.where(yh == 0, state_s[0], state_s[1])
    for c, at in enumerate(CHUNKS):
        for i in range(EARLY, NZ - 1):
            over_z(c, at, i)
    wait(weight_v, weight_sem)

    def update(at):
        product = jnp.dot(perm_v[...], dirs[:, :, :, at].reshape(R, -1), preferred_element_type=jnp.float32)
        out_v[:, at] = (weight_v[:, at].astype(jnp.float32) - 0.5 * product).astype(jnp.bfloat16)

    @pl.when(k == 1)
    def _():
        for c, at in enumerate(CHUNKS):
            for g, (first, count) in enumerate(GROUPS):
                here = dirs.at[pl.ds(first, count), :, :, at]
                wait(here, f_recv.at[c, g])
                send(here, here, pass_send, pass_recv.at[c], at_zk(0, 1))
            wait(dirs.at[0, 0, :, at], own_recv.at[c])
            update(at)
        wait(dirs.at[pl.ds(1, NZ - 1)], pass_send)

    @pl.when(k == 0)
    def _():
        for c, at in enumerate(CHUNKS):
            wait(dirs.at[0, 0, :, at], own_recv.at[c])
            wait(dirs.at[pl.ds(1, NZ - 1), :, :, at], pass_recv.at[c])
            update(at)

    wait(far_a.at[pl.ds(0, len(FAR) * NK)], far_sem.at[0])
    wait(near_a.at[pl.ds(0, len(NEAR) * NK + 1)], near_sem.at[0])
    wait(mv.at[0], mv_sem.at[0])
    wait(recv_b.at[pl.ds(0, NY - 1)], b_sem.at[0])
    wait(send_d, d_send)
    wait(dirs.at[pl.ds(0, NZ - 1), 0], f_send)
    wait(dirs.at[0, 0], own_send)


def store(weight, state, new_weight, new_moment, new_second, out_sem):
    copies = [
        pltpu.make_async_copy(weight, new_weight, out_sem.at[0]),
        pltpu.make_async_copy(state.at[0], new_moment, out_sem.at[1]),
        pltpu.make_async_copy(state.at[1], new_second, out_sem.at[2]),
    ]
    for copy in copies:
        copy.start()
    for copy in copies:
        copy.wait()


def per_device(activations, out_grads, projector, weight, moment, second):
    any_space = pl.BlockSpec(memory_space=pl.ANY)
    vmem = pl.BlockSpec(memory_space=pltpu.VMEM)
    held = pl.pallas_call(
        kernel,
        out_shape=(
            pltpu.VMEM((256, COLS), jnp.bfloat16),
            pltpu.VMEM((2, OWN, COLS), jnp.float32),
        ),
        in_specs=[any_space] * 6,
        out_specs=[vmem] * 2,
        scratch_shapes=[
            pltpu.VMEM((TOK + R, R), jnp.bfloat16),
            pltpu.VMEM((256, R), jnp.bfloat16),
            pltpu.VMEM((256, COLS), jnp.bfloat16),
            pltpu.VMEM((NX, 512, COLS), jnp.bfloat16),
            pltpu.VMEM((NYH, 2, OWN, COLS), jnp.float32),
            pltpu.VMEM((NQ, NYH * OWN, TOK), jnp.float32),
            pltpu.VMEM((NQ, NYH * OWN, TOK), jnp.bfloat16),
            pltpu.VMEM((len(NEAR) * NK + 1, NYH * OWN, TOK), jnp.float32),
            pltpu.VMEM((len(FAR) * NK, NYH * OWN, TOK), jnp.bfloat16),
            pltpu.VMEM((NY, NYH * OWN, TOK), jnp.float32),
            pltpu.VMEM((NX - 1, NYH * OWN, COLS), jnp.float32),
            pltpu.VMEM((NX - 1, NYH * OWN, COLS), jnp.float32),
            pltpu.VMEM((NYH * OWN, COLS), jnp.float32),
            pltpu.VMEM((NZ, NK, NYH * OWN, COLS), jnp.bfloat16),
            *[pltpu.SemaphoreType.DMA(())] * 4,
            *[pltpu.SemaphoreType.DMA((2,))] * 4,
            pltpu.SemaphoreType.DMA(()),
            pltpu.SemaphoreType.DMA((len(CHUNKS),)),
            pltpu.SemaphoreType.DMA(()),
            pltpu.SemaphoreType.DMA((len(CHUNKS), len(GROUPS))),
            pltpu.SemaphoreType.DMA(()),
            pltpu.SemaphoreType.DMA((len(CHUNKS),)),
            pltpu.SemaphoreType.DMA(()),
            pltpu.SemaphoreType.DMA((len(CHUNKS),)),
        ],
        compiler_params=pltpu.CompilerParams(
            collective_id=0, has_side_effects=True, vmem_limit_bytes=56 * 1024 * 1024
        ),
        name="directions",
    )(activations, out_grads, projector, weight, moment, second)
    return pl.pallas_call(
        store,
        out_shape=(
            jax.ShapeDtypeStruct(weight.shape, jnp.bfloat16),
            jax.ShapeDtypeStruct(moment.shape, jnp.float32),
            jax.ShapeDtypeStruct(second.shape, jnp.float32),
        ),
        in_specs=[vmem] * 2,
        out_specs=[any_space] * 3,
        scratch_shapes=[pltpu.SemaphoreType.DMA((3,))],
        compiler_params=pltpu.CompilerParams(vmem_limit_bytes=4 * 1024 * 1024),
        name="store",
    )(*held)


def solution(mesh):
    in_specs = (
        P("dp", "row"),
        P("dp", "col"),
        P("row", None),
        P("row", ("col", "dp")),
        P("row", ("col", "dp")),
        P("row", ("col", "dp")),
    )
    out_specs = (P("row", ("col", "dp")), P("row", ("col", "dp")), P("row", ("col", "dp")))
    return jax.shard_map(
        per_device, mesh=mesh, in_specs=in_specs, out_specs=out_specs, check_vma=False
    )
```

```python
import jax
import jax.numpy as jnp
from jax import lax
from jax.experimental import pallas as pl
from jax.experimental.pallas import tpu as pltpu
from jax.sharding import PartitionSpec as P

MESH = pl.DeviceIdType.MESH
NZ, NK, NYH, NYL, NX = 8, 2, 2, 4, 4
NQ, NY = NZ * NK, NYH * NYL
OWN = 8
TOK = 128
R = 256
COLS = 896
CHUNKS = (pl.ds(0, 512), pl.ds(512, 384))
FAR_FIRST = (4, 3, 5, 2, 6, 1, 7)
FAR, NEAR = FAR_FIRST[:5], FAR_FIRST[5:]
EARLY = 2
GROUPS = ((1, 3), (4, 4))
FIRST_FIX = 1.0 / (1.0 - 0.9**10)
SECOND_FIX = 1.0 / (1.0 - 0.999**10)


def other(i, me, n):
    return (i + (i - me + n) // n - me + n) % n


def kernel(
    act, grads, proj, weight, moment, second,
    out_v, state_v,
    first_v, perm_v, weight_v, grads_v, mv, near_a, far_a, got_near_a, got_far_a, recv_b, send_d, recv_d, low_v, dirs,
    first_sem, mv_in_sem, grads_sem, weight_sem, mv_sem, near_sem, far_sem, b_sem, d_send, d_recv, f_send, f_recv,
    own_send, own_recv, pass_send, pass_recv,
):
    row, col, dp = lax.axis_index("row"), lax.axis_index("col"), lax.axis_index("dp")
    yh, z, k = row // NQ, (row // NK) % NZ, row % NK
    y, q = yh * NYL + col, row % NQ

    def at_zk(dz, dk):
        return (yh * NQ + ((z + dz) % NZ) * NK + (k + dk) % NK, col, dp)

    def at_y(dy):
        to = (y + dy) % NY
        return ((to // NYL) * NQ + q, to % NYL, dp)

    def at_x(dx):
        return (row, col, (dp + dx) % NX)

    def send(source, target, send_sem, recv_sem, to):
        copy = pltpu.make_async_remote_copy(
            src_ref=source, dst_ref=target, send_sem=send_sem, recv_sem=recv_sem, device_id=to, device_id_type=MESH
        )
        copy.start()

    def wait(ref, sem):
        pltpu.make_async_copy(ref, ref, sem).wait()

    barrier = pltpu.get_barrier_semaphore()
    peers = []
    for far in FAR_FIRST:
        peers += [at_zk(far, 1), at_zk(far, 0), at_y(far)] + ([at_x(far)] if far < NX else [])
    peers.append(at_zk(0, 1))
    for peer in peers:
        pl.semaphore_signal(barrier, inc=1, device_id=peer, device_id_type=MESH)

    tokens = pl.ds(pl.multiple_of(col * TOK, TOK), TOK)
    pltpu.make_async_copy(act.at[tokens, :], first_v.at[pl.ds(0, TOK), :], first_sem).start()
    pltpu.make_async_copy(proj, first_v.at[pl.ds(TOK, R), :], first_sem).start()
    pltpu.make_async_copy(moment, mv.at[yh, 0], mv_in_sem).start()
    pltpu.make_async_copy(second, mv.at[yh, 1], mv_in_sem).start()
    for x in range(NX):
        pltpu.make_async_copy(grads.at[:, pl.ds(x * COLS, COLS)], grads_v.at[x], grads_sem).start()
    pltpu.make_async_copy(weight, weight_v, weight_sem).start()

    wait(first_v, first_sem)
    block = first_v[TOK:]
    part = lax.dot_general(block, first_v[:TOK], (((0,), (1,)), ((), ())), preferred_element_type=jnp.float32)
    part = part.reshape(NYH, NQ, OWN, TOK)
    part = jnp.concatenate([part[0], part[1]], axis=1)
    near_a[...] = part
    far_a[...] = part.astype(jnp.bfloat16)

    pl.semaphore_wait(barrier, len(peers))

    for i, (dz, dk) in enumerate([(dz, dk) for dz in FAR for dk in range(NK)]):
        to = ((z + dz) % NZ) * NK + (k + dk) % NK
        send(far_a.at[to], got_far_a.at[i], far_sem.at[0], far_sem.at[1], at_zk(dz, dk))
    for i, (dz, dk) in enumerate([(dz, dk) for dz in NEAR for dk in range(NK)] + [(0, 1)]):
        to = ((z + dz) % NZ) * NK + (k + dk) % NK
        send(near_a.at[to], got_near_a.at[i], near_sem.at[0], near_sem.at[1], at_zk(dz, dk))

    source = lax.broadcasted_iota(jnp.int32, (R, R), 0)
    place = lax.broadcasted_iota(jnp.int32, (R, R), 1)
    step, core, half, rank = place // (R // NZ), place // (NYH * OWN) % NK, place // OWN % NYH, place % OWN
    from_z = (z + NZ - jnp.where(step % 2 == 1, (step + 1) // 2, (NZ - step // 2) % NZ)) % NZ
    wanted = ((half * NZ + from_z) * NK + core) * OWN + rank
    shuffle = jnp.where(source == wanted, 1.0, 0.0).astype(jnp.bfloat16)
    perm_v[...] = jnp.dot(block, shuffle, preferred_element_type=jnp.float32).astype(jnp.bfloat16)

    wait(got_near_a, near_sem.at[1])
    total = near_a[q] + jnp.sum(got_near_a[...], axis=0)
    wait(got_far_a, far_sem.at[1])
    total += jnp.sum(got_far_a[...].astype(jnp.float32), axis=0)

    recv_b[y] = total
    for dy in [other(i, y, NY) for i in range(NY - 1)]:
        send(recv_b.at[y], recv_b.at[y], b_sem.at[0], b_sem.at[1], at_y(dy))

    wait(mv.at[yh], mv_in_sem)
    send(mv.at[yh], mv.at[yh], mv_sem.at[0], mv_sem.at[1], at_y(NYL))

    wait(grads_v, grads_sem)
    wait(recv_b.at[pl.ds(0, NY - 1)], b_sem.at[1])
    coords = jnp.concatenate([recv_b[c] + recv_b[NYL + c] for c in range(NYL)], axis=1)
    high = coords.astype(jnp.bfloat16)
    rest = (coords - high.astype(jnp.float32)).astype(jnp.bfloat16)
    both = jnp.concatenate([high, rest], axis=0)

    def low_of(to, at):
        product = jnp.dot(both, grads_v[to, :, at], preferred_element_type=jnp.float32)
        return product[: NYH * OWN] + product[NYH * OWN :]

    for c, at in enumerate(CHUNKS):
        for j in range(NX - 1):
            dx = other(j, dp, NX)
            send_d[j, :, at] = low_of((dp + dx) % NX, at)
            send(send_d.at[j, :, at], recv_d.at[dx - 1, :, at], d_send, d_recv.at[c], at_x(dx))
    for at in CHUNKS:
        low_v[:, at] = low_of(dp, at)
    wait(mv.at[yh], mv_sem.at[1])

    def over_z(c, at, i):
        dz = other(i, z, NZ)
        back = dz // (NZ // 2 + 1)
        slot = (2 * dz - 1) * (1 - back) + (2 * NZ - 2 * dz) * back
        send(dirs.at[0, k, :, at], dirs.at[slot, k, :, at], f_send, f_recv.at[c, slot // 4], at_zk(dz, 1 - k))

    states = []
    for c, at in enumerate(CHUNKS):
        wait(recv_d.at[:, :, at], d_recv.at[c])
        low = low_v[:, at] + recv_d[0, :, at] + recv_d[1, :, at] + recv_d[2, :, at]
        low = (low * (1.0 / NX)).reshape(NYH, OWN, -1)
        state_m = 0.9 * mv[:, 0, :, at] + 0.1 * low
        state_s = 0.999 * mv[:, 1, :, at] + 0.001 * low * low
        direction = state_m * FIRST_FIX / (jnp.sqrt(state_s * SECOND_FIX) + 1e-08)
        dirs[0, k, :, at] = direction.reshape(NYH * OWN, -1).astype(jnp.bfloat16)
        own = dirs.at[0, k, :, at]
        send(own, own, own_send, own_recv.at[c], at_zk(0, 1))
        for i in range(EARLY):
            over_z(c, at, i)
        states.append((state_m, state_s))
    for c, at in enumerate(CHUNKS):
        for i in range(EARLY, NZ - 1):
            over_z(c, at, i)
    for at, (state_m, state_s) in zip(CHUNKS, states, strict=True):
        state_v[0, :, at] = jnp.where(yh == 0, state_m[0], state_m[1])
        state_v[1, :, at] = jnp.where(yh == 0, state_s[0], state_s[1])
    wait(weight_v, weight_sem)

    def update(at):
        product = jnp.dot(perm_v[...], dirs[:, :, :, at].reshape(R, -1), preferred_element_type=jnp.float32)
        out_v[:, at] = (weight_v[:, at].astype(jnp.float32) - 0.5 * product).astype(jnp.bfloat16)

    @pl.when(k == 1)
    def _():
        for c, at in enumerate(CHUNKS):
            for g, (first, count) in enumerate(GROUPS):
                here = dirs.at[pl.ds(first, count), :, :, at]
                wait(here, f_recv.at[c, g])
                send(here, here, pass_send, pass_recv.at[c], at_zk(0, 1))
            wait(dirs.at[0, 0, :, at], own_recv.at[c])
            update(at)
        wait(dirs.at[pl.ds(1, NZ - 1)], pass_send)

    @pl.when(k == 0)
    def _():
        for c, at in enumerate(CHUNKS):
            wait(dirs.at[0, 0, :, at], own_recv.at[c])
            wait(dirs.at[pl.ds(1, NZ - 1), :, :, at], pass_recv.at[c])
            update(at)

    wait(far_a.at[pl.ds(0, len(FAR) * NK)], far_sem.at[0])
    wait(near_a.at[pl.ds(0, len(NEAR) * NK + 1)], near_sem.at[0])
    wait(mv.at[0], mv_sem.at[0])
    wait(recv_b.at[pl.ds(0, NY - 1)], b_sem.at[0])
    wait(send_d, d_send)
    wait(dirs.at[pl.ds(0, NZ - 1), 0], f_send)
    wait(dirs.at[0, 0], own_send)


def store(weight, state, new_weight, new_moment, new_second, out_sem):
    copies = [
        pltpu.make_async_copy(weight, new_weight, out_sem.at[0]),
        pltpu.make_async_copy(state.at[0], new_moment, out_sem.at[1]),
        pltpu.make_async_copy(state.at[1], new_second, out_sem.at[2]),
    ]
    for copy in copies:
        copy.start()
    for copy in copies:
        copy.wait()


def per_device(activations, out_grads, projector, weight, moment, second):
    any_space = pl.BlockSpec(memory_space=pl.ANY)
    vmem = pl.BlockSpec(memory_space=pltpu.VMEM)
    held = pl.pallas_call(
        kernel,
        out_shape=(
            pltpu.VMEM((256, COLS), jnp.bfloat16),
            pltpu.VMEM((2, OWN, COLS), jnp.float32),
        ),
        in_specs=[any_space] * 6,
        out_specs=[vmem] * 2,
        scratch_shapes=[
            pltpu.VMEM((TOK + R, R), jnp.bfloat16),
            pltpu.VMEM((256, R), jnp.bfloat16),
            pltpu.VMEM((256, COLS), jnp.bfloat16),
            pltpu.VMEM((NX, 512, COLS), jnp.bfloat16),
            pltpu.VMEM((NYH, 2, OWN, COLS), jnp.float32),
            pltpu.VMEM((NQ, NYH * OWN, TOK), jnp.float32),
            pltpu.VMEM((NQ, NYH * OWN, TOK), jnp.bfloat16),
            pltpu.VMEM((len(NEAR) * NK + 1, NYH * OWN, TOK), jnp.float32),
            pltpu.VMEM((len(FAR) * NK, NYH * OWN, TOK), jnp.bfloat16),
            pltpu.VMEM((NY, NYH * OWN, TOK), jnp.float32),
            pltpu.VMEM((NX - 1, NYH * OWN, COLS), jnp.float32),
            pltpu.VMEM((NX - 1, NYH * OWN, COLS), jnp.float32),
            pltpu.VMEM((NYH * OWN, COLS), jnp.float32),
            pltpu.VMEM((NZ, NK, NYH * OWN, COLS), jnp.bfloat16),
            *[pltpu.SemaphoreType.DMA(())] * 4,
            *[pltpu.SemaphoreType.DMA((2,))] * 4,
            pltpu.SemaphoreType.DMA(()),
            pltpu.SemaphoreType.DMA((len(CHUNKS),)),
            pltpu.SemaphoreType.DMA(()),
            pltpu.SemaphoreType.DMA((len(CHUNKS), len(GROUPS))),
            pltpu.SemaphoreType.DMA(()),
            pltpu.SemaphoreType.DMA((len(CHUNKS),)),
            pltpu.SemaphoreType.DMA(()),
            pltpu.SemaphoreType.DMA((len(CHUNKS),)),
        ],
        compiler_params=pltpu.CompilerParams(
            collective_id=0, has_side_effects=True, vmem_limit_bytes=56 * 1024 * 1024
        ),
        name="directions",
    )(activations, out_grads, projector, weight, moment, second)
    return pl.pallas_call(
        store,
        out_shape=(
            jax.ShapeDtypeStruct(weight.shape, jnp.bfloat16),
            jax.ShapeDtypeStruct(moment.shape, jnp.float32),
            jax.ShapeDtypeStruct(second.shape, jnp.float32),
        ),
        in_specs=[vmem] * 2,
        out_specs=[any_space] * 3,
        scratch_shapes=[pltpu.SemaphoreType.DMA((3,))],
        compiler_params=pltpu.CompilerParams(vmem_limit_bytes=4 * 1024 * 1024),
        name="store",
    )(*held)


def solution(mesh):
    in_specs = (
        P("dp", "row"),
        P("dp", "col"),
        P("row", None),
        P("row", ("col", "dp")),
        P("row", ("col", "dp")),
        P("row", ("col", "dp")),
    )
    out_specs = (P("row", ("col", "dp")), P("row", ("col", "dp")), P("row", ("col", "dp")))
    return jax.shard_map(
        per_device, mesh=mesh, in_specs=in_specs, out_specs=out_specs, check_vma=False
    )
```
